512 devices in a mesh: sub: 32 (over z_lo, y, core), cr: 4 (over x), cc: 4 (over z_hi).
Axes of the slice: x: 4, y: 4, z: 16 (z_hi: 4, z_lo: 4; z = z_hi * 4 + z_lo), core: 2. Of those that a mesh axis runs over, the one named last changes fastest.
Arguments:
- stiffness: bfloat16 [128, 1536, 1536], P(('sub', 'cr'), 'cc')
- local_inverse: bfloat16 [128, 1536, 1536], P(('sub', 'cr'), 'cc')
- coarse_basis: bfloat16 [128, 64, 1536], P(('sub', 'cr'), None, 'cc'), may hold values from -0.15625 to 0.15625
- coarse_inverse: bfloat16 [128, 64, 64, 128], P(('sub', 'cr'), None, 'cc')
- loads: float32 [128, 1536, 256], P(('sub', 'cr'), 'cc'), may hold values from -6 to 6
- initial: float32 [128, 1536, 256], P(('sub', 'cr'), 'cc'), may hold values from -6 to 6
- margin_rows: int32 [128, 2, 128], P(('sub', 'cr')), may hold values from 0 to 1535, as said below
- coarse_map: int32 [128], replicated, may hold values from 0 to 127, as said below
Outputs:
- solution: float32 [128, 1536, 256], P(('sub', 'cr'), 'cc')
- residual: float32 [128, 1536, 256], P(('sub', 'cr'), 'cc')
The draws below stay inside these ranges and needn't reach their ends.
Inputs may be any that keep to these rules, and one draw needn't show every extreme that they name: `margin_rows`: the 256 row numbers of one subdomain are distinct. `coarse_map`: every coarse block number appears once.
All inputs are finite; a program needn't handle non-finite values.
Results may differ from the reference program's by a relative error of at most 0.0095.
Values may be sent and summed in bfloat16 or wider, within the bound.
A program may use at most 64 MiB of HBM per device.

```python
import jax
import jax.numpy as jnp
from jax import lax

BLOCK = 1536
COARSE = 64
RHS = 256
MARGIN = 128
ITERS = 2
SUBDOMAINS = 128


def stiff_diagonal(key):
    return jnp.exp(jax.random.uniform(jax.random.fold_in(key, 5), (SUBDOMAINS, BLOCK), jnp.float32) * jnp.log(4.0))


def block_order(key):
    return jax.random.permutation(jax.random.fold_in(key, 7), SUBDOMAINS)


def draw_stiffness(key, part):
    diagonal = stiff_diagonal(key)
    key = jax.random.fold_in(key, 21)
    jitter = jax.random.truncated_normal(key, -4.0, 4.0, (SUBDOMAINS, BLOCK, BLOCK), jnp.float32)
    identity = jnp.eye(BLOCK, dtype=jnp.float32)
    return (jitter * (0.6 / BLOCK ** 0.5) + identity * diagonal[:, :, None]).astype(jnp.bfloat16)


def draw_local_inverse(key, part):
    diagonal = stiff_diagonal(key)
    key = jax.random.fold_in(key, 23)
    key_one, key_two = jax.random.split(key)
    damping = jnp.exp(jax.random.uniform(key_one, (SUBDOMAINS, BLOCK), jnp.float32, jnp.log(0.6), 0.0))
    jitter = jax.random.truncated_normal(key_two, -4.0, 4.0, (SUBDOMAINS, BLOCK, BLOCK), jnp.float32)
    identity = jnp.eye(BLOCK, dtype=jnp.float32)
    return (jitter * (0.8 / BLOCK ** 0.5) + identity * (damping / diagonal)[:, :, None]).astype(jnp.bfloat16)


def draw_coarse_inverse(key, part):
    ordering = block_order(key)
    key = jax.random.fold_in(key, 31)
    key_one, key_two = jax.random.split(key)
    strength = 2.0 * jnp.exp(jax.random.uniform(key_one, (SUBDOMAINS, COARSE), jnp.float32) * jnp.log(4.0))
    shape_full = (SUBDOMAINS, COARSE, COARSE, SUBDOMAINS)
    jitter = jax.random.truncated_normal(key_two, -4.0, 4.0, shape_full, jnp.float32)
    selector = (jnp.arange(SUBDOMAINS)[None, :] == ordering[:, None]).astype(jnp.float32)
    identity = jnp.eye(COARSE, dtype=jnp.float32)
    dominant = strength[:, :, None, None] * identity[None, :, :, None] * selector[:, None, None, :]
    return (jitter * (1.5 / (COARSE * SUBDOMAINS) ** 0.5) + dominant).astype(jnp.bfloat16)


def draw_coarse_map(key, part):
    ordering = block_order(key)
    return ordering.astype(jnp.int32)


def draw_margin_rows(key, part):
    key = jax.random.fold_in(key, 13)
    subkeys = jax.random.split(key, SUBDOMAINS)
    picked = jax.vmap(lambda single: jax.random.permutation(single, BLOCK)[:2 * MARGIN])(subkeys)
    return picked.reshape(SUBDOMAINS, 2, MARGIN).astype(jnp.int32)


def block_scale(stream_key, extent, cuts, smallest, high):
    def one(dim, blocks):
        heights = jax.random.uniform(jax.random.fold_in(jax.random.fold_in(stream_key, 6), dim), (blocks,), jnp.float32, smallest / len(cuts), high / len(cuts))
        return jnp.repeat(jnp.exp(heights), extent[dim] // blocks).reshape((-1,) + (1,) * (len(extent) - dim - 1))

    gain = one(*cuts[0])
    for cut in cuts[1:]:
        gain = gain * one(*cut)
    return gain


def bell_draw(key, shape, width, bound, cuts=(), kind=jnp.bfloat16):
    result = jax.random.normal(key, shape, jnp.float32) * width
    if len(cuts) > 0:
        result = block_scale(key, shape, cuts, -0.22, 0.18) * result
    return jnp.clip(result, min=-bound, max=bound).astype(kind)


def setup_inputs(seed: int = 0) -> dict:
    arg_keys = jax.random.split(jax.random.key(seed), 9)
    return {
        "stiffness": draw_stiffness(jax.random.fold_in(arg_keys[8], 71), 0),
        "local_inverse": draw_local_inverse(jax.random.fold_in(arg_keys[8], 71), 0),
        "coarse_basis": bell_draw(arg_keys[2], (SUBDOMAINS, COARSE, BLOCK), BLOCK ** -0.5, 0.15625, ((0, 128), (2, 4))),
        "coarse_inverse": draw_coarse_inverse(jax.random.fold_in(arg_keys[8], 71), 0),
        "loads": bell_draw(arg_keys[4], (SUBDOMAINS, BLOCK, RHS), 1.0, 6.0, ((0, 128), (1, 4)), jnp.float32),
        "initial": bell_draw(arg_keys[5], (SUBDOMAINS, BLOCK, RHS), 1.0, 6.0, ((0, 128), (1, 4)), jnp.float32),
        "margin_rows": draw_margin_rows(jax.random.fold_in(arg_keys[8], 71), 0),
        "coarse_map": draw_coarse_map(jax.random.fold_in(arg_keys[8], 71), 0),
    }


RELAX = 0.5


def block_products(matrices, vectors):
    def single(operands):
        return jnp.dot(operands[0], operands[1], preferred_element_type=jnp.float32)
    return lax.map(single, (matrices, vectors))


def basis_products(basis, coarse_values):
    def single(operands):
        return jnp.dot(operands[0].T, operands[1], preferred_element_type=jnp.float32)
    return lax.map(single, (basis, coarse_values))


def assemble(values, margin_rows):
    left_index = margin_rows[:, 0, :]
    right_index = margin_rows[:, 1, :]
    outgoing_up = jax.vmap(lambda source, indices: source[indices])(values, right_index)
    outgoing_down = jax.vmap(lambda source, indices: source[indices])(values, left_index)
    padding = jnp.zeros_like(outgoing_up[:1])
    from_below = jnp.concatenate([padding, outgoing_up[:-1]], axis=0)
    from_above = jnp.concatenate([outgoing_down[1:], padding], axis=0)

    def place_rows(target, left_at, right_at, lower, upper):
        return target.at[left_at].add(lower).at[right_at].add(upper)

    return jax.vmap(place_rows)(values, left_index, right_index, from_below, from_above)


def residual_of(solution, loads, stiffness, margin_rows):
    product = block_products(stiffness, solution.astype(jnp.bfloat16))
    return assemble(loads - product, margin_rows)


def reference(stiffness, local_inverse, coarse_basis, coarse_inverse, loads, initial, margin_rows, coarse_map):
    subdomain_count = coarse_map.shape[0]
    ordered = jnp.take(coarse_inverse, coarse_map, axis=3).reshape(subdomain_count * COARSE, COARSE * subdomain_count)
    solution = initial
    for iteration in range(ITERS):
        defect = residual_of(solution, loads, stiffness, margin_rows)
        rounded = defect.astype(jnp.bfloat16)
        coarse_defect = block_products(coarse_basis, rounded).astype(jnp.bfloat16)
        stacked = jnp.transpose(coarse_defect, (1, 0, 2)).reshape(COARSE * subdomain_count, RHS)
        coarse_value = jnp.dot(ordered, stacked, preferred_element_type=jnp.float32)
        coarse_value = coarse_value.reshape(subdomain_count, COARSE, RHS).astype(jnp.bfloat16)
        local_part = block_products(local_inverse, rounded)
        correction = assemble(local_part + basis_products(coarse_basis, coarse_value), margin_rows)
        solution = solution + RELAX * correction
    return solution, residual_of(solution, loads, stiffness, margin_rows)
```

```python
import functools

import jax
import jax.numpy as jnp
from jax import lax
from jax.experimental import pallas as pl
from jax.experimental.pallas import tpu as pltpu
from jax.sharding import PartitionSpec as P

COARSE = 64
ITERS = 2
RELAX = 0.5
PARTS = 1
SUB_EXTENTS = (4, 4, 2)
RING = 4
MESH = pl.DeviceIdType.MESH
BF16 = jnp.bfloat16
F32 = jnp.float32


def dot(a, b):
    return jnp.dot(a, b, preferred_element_type=F32)


def dot_nt(a, b):
    return lax.dot_general(a, b, (((1,), (1,)), ((), ())), preferred_element_type=F32)


def kernel(
    extents,
    stiff_hbm,
    inverse_hbm,
    basis_ref,
    weight_ref,
    load_ref,
    init_ref,
    row_ref,
    col_ref,
    sol_ref,
    res_ref,
    k_buf,
    a_buf,
    p_buf,
    pt_buf,
    ap_buf,
    kp_buf,
    bp_buf,
    pb_buf,
    kb_buf,
    bt_buf,
    basis_buf,
    gathered,
    defect,
    update,
    picked,
    coarse_acc,
    margin_out,
    margin_in,
    coarse_all,
    value_out,
    value_own,
    value_in,
    value_all,
    final_out,
    final_in,
    final_sum,
    final_near,
    final_all,
    local_sem,
    send_sem,
    recv_sem,
):
    nz, ny, nc, nx = extents
    own, block = stiff_hbm.shape
    width = load_ref.shape[1] // PARTS
    margin = row_ref.shape[1] // 2
    quarter = COARSE // RING
    piece = margin // RING
    sub = lax.axis_index("sub")
    x = lax.axis_index("cr")
    j = lax.axis_index("cc")
    z = sub // (ny * nc)
    y = lax.rem(sub // nc, ny)
    c = lax.rem(sub, nc)
    domain = sub * nx + x
    domains = nz * ny * nc * nx

    def device(zz, yy, cc, xx, jj):
        return ((zz * ny + yy) * nc + cc, xx, jj)

    def ring(delta):
        return lax.rem(j + delta, RING)

    def ring_device(delta):
        return device(z, y, c, x, ring(delta))

    def domain_device(delta):
        other = lax.rem(domain + delta + domains, domains)
        return (other // nx, lax.rem(other, nx), j)

    axes = {
        "z": (nz, z, lambda v: device(v, y, c, x, j)),
        "y": (ny, y, lambda v: device(z, v, c, x, j)),
        "x": (nx, x, lambda v: device(z, y, c, v, j)),
        "c": (nc, c, lambda v: device(z, y, v, x, j)),
    }

    partners = [ring_device(d) for d in range(1, RING)]
    partners += [domain_device(1), domain_device(-1)]
    for extent, mine, at in axes.values():
        partners += [at(lax.rem(mine + d, extent)) for d in range(1, extent)]

    loads_of_matrices = []
    for jj in range(RING):
        for n, (source, target) in enumerate(((stiff_hbm, k_buf), (inverse_hbm, a_buf))):
            copy = pltpu.make_async_copy(
                source.at[:, pl.ds(jj * own, own)], target.at[jj], local_sem.at[2 * jj + n]
            )
            copy.start()
            loads_of_matrices.append(copy)

    barrier = pltpu.get_barrier_semaphore()
    for partner in partners:
        pl.semaphore_signal(barrier, inc=1, device_id=partner, device_id_type=MESH)
    pl.semaphore_wait(barrier, len(partners))

    slots = [0]
    started = []

    def reserve(count):
        first = slots[0]
        slots[0] += count
        return first

    def remote(source, target, slot, to):
        return pltpu.make_async_remote_copy(
            src_ref=source,
            dst_ref=target,
            send_sem=send_sem.at[slot],
            recv_sem=recv_sem.at[slot],
            device_id=to,
            device_id_type=MESH,
        )

    def send(source, target, slot, to):
        copy = remote(source, target, slot, to)
        copy.start()
        started.append(copy)

    def arrive(landed, slot):
        remote(landed, landed, slot, ring_device(1)).wait_recv()

    class Gather:
        def __init__(self, ref, rows):
            self.ref, self.half, self.slot = ref, rows // 2, reserve(6)

        def at(self, delta, half):
            return self.ref.at[ring(delta), pl.ds(half * self.half, self.half)]

        def start(self):
            right, left, s = ring_device(1), ring_device(3), self.slot
            send(self.at(0, 0), self.at(0, 0), s, right)
            send(self.at(0, 1), self.at(0, 1), s + 1, left)
            send(self.at(0, 1), self.at(0, 1), s + 2, right)
            send(self.at(0, 0), self.at(0, 0), s + 3, left)

        def forward(self):
            s = self.slot
            arrive(self.at(3, 0), s)
            send(self.at(3, 0), self.at(3, 0), s + 4, ring_device(1))
            arrive(self.at(1, 1), s + 1)
            send(self.at(1, 1), self.at(1, 1), s + 5, ring_device(3))

        def near(self):
            arrive(self.at(3, 1), self.slot + 2)
            arrive(self.at(1, 0), self.slot + 3)

        def far(self):
            arrive(self.at(2, 0), self.slot + 4)
            arrive(self.at(2, 1), self.slot + 5)

    def swap(name, ref_at):
        extent, mine, at = axes[name]
        first = reserve(max(extent - 1, 0))
        for d in range(1, extent):
            send(ref_at(mine), ref_at(mine), first + d - 1, at(lax.rem(mine + d, extent)))

        def wait():
            for d in range(1, extent):
                arrive(ref_at(lax.rem(mine + extent - d, extent)), first + d - 1)

        return wait

    def columns(h):
        return slice(h * width, (h + 1) * width)

    def one_hots():
        for jj in range(RING):
            lane = lax.broadcasted_iota(jnp.int32, (2 * margin, own), 1) + jj * own
            p_buf[jj] = jnp.where(col_ref[...] == lane, 1.0, 0.0).astype(BF16)
            row = lax.broadcasted_iota(jnp.int32, (own, 2 * margin), 0) + jj * own
            pt_buf[jj] = jnp.where(row_ref[...] == row, 1.0, 0.0).astype(BF16)

    def margin_columns():
        for source, target in ((k_buf, kp_buf), (a_buf, ap_buf)):
            total = dot(source[0], pt_buf[0])
            for jj in range(1, RING):
                total += dot(source[jj], pt_buf[jj])
            target[...] = total.astype(BF16)

    def own_basis():
        row = lax.broadcasted_iota(jnp.int32, (own, own), 0)
        col = lax.broadcasted_iota(jnp.int32, (own, own), 1)
        identity = jnp.where(row == col, 1.0, 0.0).astype(BF16)
        bt_buf[...] = dot_nt(identity, basis_ref[...]).astype(BF16)

    def basis_rows(jj):
        return basis_buf[jj, pl.ds(pl.multiple_of(j * quarter, quarter), quarter), :]

    def basis_terms():
        total = jnp.zeros((own, COARSE), F32)
        shared = jnp.zeros((2 * margin, COARSE), F32)
        rows = jnp.zeros((quarter, 2 * margin), F32)
        for jj in range(RING):
            total += dot_nt(k_buf[jj], basis_buf[jj])
            shared += dot_nt(p_buf[jj], basis_buf[jj])
            rows += dot(basis_rows(jj), pt_buf[jj])
        high = total.astype(BF16)
        kb_buf[0] = high
        kb_buf[1] = (total - high.astype(F32)).astype(BF16)
        pb_buf[...] = shared.astype(BF16)
        bp_buf[...] = rows.astype(BF16)

    def exchange_margins(step, h, values):
        margin_out[step, h, 0] = values[:margin].astype(BF16)
        margin_out[step, h, 1] = values[margin:].astype(BF16)
        first = reserve(2)
        send(margin_out.at[step, h, 1], margin_in.at[step, h, 0], first, domain_device(1))
        send(margin_out.at[step, h, 0], margin_in.at[step, h, 1], first + 1, domain_device(-1))

        def wait():
            arrive(margin_in.at[step, h, 0], first)
            arrive(margin_in.at[step, h, 1], first + 1)
            below, above = margin_in[step, h, 0], margin_in[step, h, 1]
            return masked(below, above)

        return wait

    def masked(below, above):
        zero = jnp.zeros_like(below)
        below = jnp.where(domain > 0, below, zero)
        above = jnp.where(domain < domains - 1, above, zero)
        return jnp.concatenate([below, above], axis=0)

    def process(h):
        cols = columns(h)
        start_block = gathered.at[0, h]
        gathered[0, h, j] = init_ref[:, cols].astype(BF16)
        gather = Gather(start_block, own)
        gather.start()
        if h == 0:
            for copy in loads_of_matrices:
                copy.wait()
            one_hots()
            margin_columns()
            own_basis()
        yield
        sol_ref[:, cols] = init_ref[:, cols]

        def take_start(delta):
            defect[h] -= dot(k_buf[ring(delta)], gathered[0, h, ring(delta)])

        defect[h] = load_ref[:, cols] - dot(k_buf[j], gathered[0, h, j])
        gather.forward()
        if h == 0:
            basis_gather.append(Gather(basis_buf, COARSE))
            basis_buf[j] = basis_ref[...]
            basis_gather[0].start()
        gather.near()
        take_start(3)
        take_start(1)
        if h == 0:
            basis_gather[0].forward()
        gather.far()
        take_start(2)

        for it in range(ITERS):
            level = 1 + 2 * it
            gathered[level, h, j] = defect[h].astype(BF16)
            gather = Gather(gathered.at[level, h], own)
            gather.start()
            yield
            if it == 0 and h == 0:
                basis_gather[0].near()
                basis_gather[0].far()
                basis_terms()

            def take_defect(delta, first=False, level=level):
                jj = ring(delta)
                part = gathered[level, h, jj]
                terms = (
                    (picked, dot(p_buf[jj], part)),
                    (update, dot(a_buf[jj], part)),
                    (coarse_acc, dot(basis_rows(jj), part)),
                )
                for target, term in terms:
                    if first:
                        target[h] = term
                    else:
                        target[h] += term

            take_defect(0, True)
            gather.forward()
            gather.near()
            take_defect(3)
            take_defect(1)
            gather.far()
            take_defect(2)
            margins = exchange_margins(2 * it, h, picked[h])
            yield
            shared = margins()
            result = coarse_acc[h] + dot(bp_buf[...], shared)
            coarse_all[it, h, c, x, y, z] = result.astype(BF16)
            wait_z = swap("z", lambda v: coarse_all.at[it, h, c, x, y, v])
            update[h] += dot(ap_buf[...], shared)
            level += 1
            gathered[level, h, j] = update[h].astype(BF16)
            gather = Gather(gathered.at[level, h], own)
            gather.start()
            wait_z()
            wait_y = swap("y", lambda v: coarse_all.at[it, h, c, x, v])
            yield

            def take_update(delta, first=False, level=level):
                jj = ring(delta)
                part = gathered[level, h, jj]
                term = dot(p_buf[jj], part)
                if first:
                    picked[h] = term
                else:
                    picked[h] += term
                defect[h] -= RELAX * dot(k_buf[jj], part)

            take_update(0, True)
            wait_y()
            wait_x = swap("x", lambda v: coarse_all.at[it, h, c, v])
            gather.forward()
            wait_x()
            wait_c = swap("c", lambda v: coarse_all.at[it, h, v])
            wait_c()
            everything = coarse_all[it, h].reshape(domains * quarter, width)
            partial = dot(weight_ref[...], everything).reshape(RING, quarter, width)
            value_own[h] = partial
            value_out[it, h] = partial.astype(BF16)
            first = reserve(RING - 1)
            for d in range(1, RING):
                send(
                    value_out.at[it, h, ring(d)],
                    value_in.at[it, h, d - 1],
                    first + d - 1,
                    ring_device(d),
                )
            gather.near()
            take_update(3)
            take_update(1)
            total = value_own[h, j]
            for d in range(1, RING):
                arrive(value_in.at[it, h, d - 1], first + d - 1)
                total += value_in[it, h, d - 1].astype(F32)
            value_all[it, h, j] = total.astype(BF16)
            first = reserve(RING - 1)
            for d in range(1, RING):
                send(
                    value_all.at[it, h, j], value_all.at[it, h, j], first + d - 1, ring_device(d)
                )
            gather.far()
            take_update(2)
            for d in range(1, RING):
                arrive(value_all.at[it, h, ring(RING - d)], first + d - 1)
            value = value_all[it, h].reshape(COARSE, width)
            margins = exchange_margins(2 * it + 1, h, picked[h] + dot(pb_buf[...], value))
            defect[h] -= RELAX * (dot(kb_buf[0], value) + dot(kb_buf[1], value))
            sol_ref[:, cols] += RELAX * (update[h] + dot(bt_buf[...], value))
            yield
            shared = margins()
            defect[h] -= RELAX * dot(kp_buf[...], shared)
            sol_ref[:, cols] += RELAX * dot(pt_buf[j], shared)

        mine = dot(p_buf[j], defect[h].astype(BF16))
        final_out[h, :, 0] = mine[:margin].reshape(RING, piece, width).astype(BF16)
        final_out[h, :, 1] = mine[margin:].reshape(RING, piece, width).astype(BF16)
        first = reserve(RING - 1)
        for d in range(1, RING):
            send(final_out.at[h, ring(d)], final_in.at[h, d - 1], first + d - 1, ring_device(d))
        yield
        total = final_out[h, j].astype(F32)
        for d in range(1, RING):
            arrive(final_in.at[h, d - 1], first + d - 1)
            total += final_in[h, d - 1].astype(F32)
        final_sum[h] = total.astype(BF16)
        first = reserve(2)
        send(final_sum.at[h, 1], final_all.at[h, j, 0], first, domain_device(1))
        send(final_sum.at[h, 0], final_all.at[h, j, 1], first + 1, domain_device(-1))
        yield
        arrive(final_all.at[h, j, 0], first)
        arrive(final_all.at[h, j, 1], first + 1)
        first = reserve(RING - 1)
        for d in range(1, RING):
            send(final_all.at[h, j], final_all.at[h, j], first + d - 1, ring_device(d))
        yield
        for d in range(1, RING):
            arrive(final_all.at[h, ring(RING - d)], first + d - 1)
        shared = masked(
            final_all[h, :, 0].reshape(margin, width), final_all[h, :, 1].reshape(margin, width)
        )
        res_ref[:, cols] = defect[h] + dot(pt_buf[j], shared)

    basis_gather = []
    running = [process(h) for h in range(PARTS)]
    while running:
        for item in list(running):
            try:
                next(item)
            except StopIteration:
                running.remove(item)
    for copy in started:
        copy.wait_send()


def on_device(
    stiffness, local_inverse, coarse_basis, coarse_inverse, loads, initial, margin_rows, coarse_map
):
    nz, ny, nc = SUB_EXTENTS
    nx = lax.axis_size("cr")
    own, block = stiffness.shape[1:]
    rhs = loads.shape[2]
    width = rhs // PARTS
    domains = coarse_map.shape[0]
    quarter = COARSE // RING
    margin = margin_rows.shape[2]
    piece = margin // RING
    order = jnp.transpose(coarse_map.reshape(nz, ny, nc, nx), (2, 3, 1, 0)).reshape(-1)
    ordered = jnp.take(coarse_inverse[0], order, axis=2)
    weights = jnp.transpose(ordered, (0, 2, 1)).reshape(COARSE, -1)
    rows = margin_rows[0].reshape(1, 2 * margin)
    vmem = pl.BlockSpec(memory_space=pltpu.VMEM)
    hbm = pl.BlockSpec(memory_space=pl.ANY)
    slots = 256
    result = pl.pallas_call(
        functools.partial(kernel, (nz, ny, nc, nx)),
        out_shape=(
            jax.ShapeDtypeStruct((own, rhs), F32),
            jax.ShapeDtypeStruct((own, rhs), F32),
        ),
        in_specs=[hbm, hbm] + [vmem] * 6,
        out_specs=(vmem, vmem),
        scratch_shapes=[
            pltpu.VMEM((RING, own, own), BF16),
            pltpu.VMEM((RING, own, own), BF16),
            pltpu.VMEM((RING, 2 * margin, own), BF16),
            pltpu.VMEM((RING, own, 2 * margin), BF16),
            pltpu.VMEM((own, 2 * margin), BF16),
            pltpu.VMEM((own, 2 * margin), BF16),
            pltpu.VMEM((quarter, 2 * margin), BF16),
            pltpu.VMEM((2 * margin, COARSE), BF16),
            pltpu.VMEM((2, own, COARSE), BF16),
            pltpu.VMEM((own, COARSE), BF16),
            pltpu.VMEM((RING, COARSE, own), BF16),
            pltpu.VMEM((1 + 2 * ITERS, PARTS, RING, own, width), BF16),
            pltpu.VMEM((PARTS, own, width), F32),
            pltpu.VMEM((PARTS, own, width), F32),
            pltpu.VMEM((PARTS, 2 * margin, width), F32),
            pltpu.VMEM((PARTS, quarter, width), F32),
            pltpu.VMEM((2 * ITERS, PARTS, 2, margin, width), BF16),
            pltpu.VMEM((2 * ITERS, PARTS, 2, margin, width), BF16),
            pltpu.VMEM((ITERS, PARTS, nc, nx, ny, nz, quarter, width), BF16),
            pltpu.VMEM((ITERS, PARTS, RING, quarter, width), BF16),
            pltpu.VMEM((PARTS, RING, quarter, width), F32),
            pltpu.VMEM((ITERS, PARTS, RING - 1, quarter, width), BF16),
            pltpu.VMEM((ITERS, PARTS, RING, quarter, width), BF16),
            pltpu.VMEM((PARTS, RING, 2, piece, width), BF16),
            pltpu.VMEM((PARTS, RING - 1, 2, piece, width), BF16),
            pltpu.VMEM((PARTS, 2, piece, width), BF16),
            pltpu.VMEM((PARTS, 2, piece, width), BF16),
            pltpu.VMEM((PARTS, RING, 2, piece, width), BF16),
            pltpu.SemaphoreType.DMA((2 * RING,)),
            pltpu.SemaphoreType.DMA((slots,)),
            pltpu.SemaphoreType.DMA((slots,)),
        ],
        compiler_params=pltpu.CompilerParams(
            collective_id=0, has_side_effects=True, vmem_limit_bytes=48 * 1024 * 1024
        ),
    )(
        stiffness[0],
        local_inverse[0],
        coarse_basis[0],
        weights,
        loads[0],
        initial[0],
        rows,
        rows.reshape(2 * margin, 1),
    )
    return (result[0][None], result[1][None])


def solution(mesh):
    in_specs = (
        P(("sub", "cr"), "cc", None),
        P(("sub", "cr"), "cc", None),
        P(("sub", "cr"), None, "cc"),
        P(("sub", "cr"), None, "cc", None),
        P(("sub", "cr"), "cc", None),
        P(("sub", "cr"), "cc", None),
        P(("sub", "cr"), None, None),
        P(),
    )
    out_specs = (P(("sub", "cr"), "cc", None), P(("sub", "cr"), "cc", None))
    return jax.shard_map(
        on_device, mesh=mesh, in_specs=in_specs, out_specs=out_specs, check_vma=False
    )
```

```python
import functools

import jax
import jax.numpy as jnp
from jax import lax
from jax.experimental import pallas as pl
from jax.experimental.pallas import tpu as pltpu
from jax.sharding import PartitionSpec as P

COARSE = 64
ITERS = 2
RELAX = 0.5
PARTS = 2
SUB_EXTENTS = (4, 4, 2)
RING = 4
ORDER = (
    "Ax0", "matrices", "Ax1", "Bx0", "Ax2", "Bx1", "start_basis", "weights", "Ax3", "Ae1",
    "Bx2", "forward_basis", "Ae2", "Bx3", "Ae3", "end_basis", "Be1", "Ae4", "Au1", "Be2",
    "Be3", "Au2", "Au3", "Au4", "Au5", "Be4", "Bu1", "Au6", "Au7", "Bu2",
    "Au8", "Bu3", "Bu4", "Bu5", "Au9", "Bu6", "Bu7", "Bu8", "Ae1", "Bu9",
    "Ae2", "Ae3", "Be1", "Ae4", "Be2", "Au1", "Be3", "Au2", "Au3", "Be4",
    "Au4", "Bu1", "Au5", "Au6", "Bu2", "Bu3", "Au7", "Bu4", "Bu5", "Bu6",
    "Au8", "Bu7", "Bu8", "Au9", "Bu9", "Af1", "Bf1", "Af2", "Bf2", "Af3",
    "Bf3",
)
MESH = pl.DeviceIdType.MESH
BF16 = jnp.bfloat16
F32 = jnp.float32


def dot(a, b):
    return jnp.dot(a, b, preferred_element_type=F32)


def dot_nt(a, b):
    return lax.dot_general(a, b, (((1,), (1,)), ((), ())), preferred_element_type=F32)


def kernel(
    extents,
    stiff_hbm,
    inverse_hbm,
    basis_hbm,
    coarse_hbm,
    load_hbm,
    init_hbm,
    row_ref,
    map_ref,
    sol_ref,
    res_ref,
    load_ref,
    init_ref,
    basis_ref,
    coarse_ref,
    weight_buf,
    k_buf,
    a_buf,
    p_buf,
    pt_buf,
    ap_buf,
    kp_buf,
    bp_buf,
    pb_buf,
    kb_buf,
    bt_buf,
    basis_buf,
    gathered,
    defect,
    update,
    picked,
    margin_out,
    margin_in,
    coarse_all,
    value_out,
    value_own,
    value_in,
    final_out,
    final_in,
    final_sum,
    final_near,
    final_all,
    local_sem,
    send_sem,
    recv_sem,
):
    nz, ny, nc, nx = extents
    own, block = stiff_hbm.shape
    width = load_ref.shape[1] // PARTS
    margin = row_ref.shape[1]
    quarter = COARSE // RING
    piece = margin // RING
    sub = lax.axis_index("sub")
    x = lax.axis_index("cr")
    j = lax.axis_index("cc")
    z = sub // (ny * nc)
    y = lax.rem(sub // nc, ny)
    c = lax.rem(sub, nc)
    domain = sub * nx + x
    domains = nz * ny * nc * nx

    def device(zz, yy, cc, xx, jj):
        return ((zz * ny + yy) * nc + cc, xx, jj)

    def ring(delta):
        return lax.rem(j + delta, RING)

    def ring_device(delta):
        return device(z, y, c, x, ring(delta))

    def domain_device(delta):
        other = lax.rem(domain + delta + domains, domains)
        return (other // nx, lax.rem(other, nx), j)

    axes = {
        "z": (nz, z, lambda v: device(v, y, c, x, j)),
        "y": (ny, y, lambda v: device(z, v, c, x, j)),
        "x": (nx, x, lambda v: device(z, y, c, v, j)),
        "c": (nc, c, lambda v: device(z, y, v, x, j)),
    }

    partners = [ring_device(d) for d in range(1, RING)]
    partners += [domain_device(1), domain_device(-1)]
    for extent, mine, at in axes.values():
        partners += [at(lax.rem(mine + d, extent)) for d in range(1, extent)]

    copies = []

    def fetch(source, target):
        copy = pltpu.make_async_copy(source, target, local_sem.at[len(copies)])
        copy.start()
        copies.append(copy)

    barrier = pltpu.get_barrier_semaphore()
    for partner in partners:
        pl.semaphore_signal(barrier, inc=1, device_id=partner, device_id_type=MESH)
    fetch(init_hbm, init_ref)
    fetch(load_hbm, load_ref)
    fetch(basis_hbm, basis_ref)
    for source, target in ((stiff_hbm, k_buf), (inverse_hbm, a_buf)):
        for jj in range(RING):
            fetch(source.at[:, pl.ds(jj * own, own)], target.at[jj])
    fetch(coarse_hbm, coarse_ref)

    slots = [0]
    started = []

    def reserve(count):
        first = slots[0]
        slots[0] += count
        return first

    def remote(source, target, slot, to):
        return pltpu.make_async_remote_copy(
            src_ref=source,
            dst_ref=target,
            send_sem=send_sem.at[slot],
            recv_sem=recv_sem.at[slot],
            device_id=to,
            device_id_type=MESH,
        )

    def send(source, target, slot, to):
        copy = remote(source, target, slot, to)
        copy.start()
        started.append(copy)

    def arrive(landed, slot):
        remote(landed, landed, slot, ring_device(1)).wait_recv()

    class Gather:
        def __init__(self, ref, rows):
            self.ref, self.half, self.slot = ref, rows // 2, reserve(6)

        def at(self, delta, half):
            return self.ref.at[ring(delta), pl.ds(half * self.half, self.half)]

        def start(self):
            right, left, s = ring_device(1), ring_device(3), self.slot
            send(self.at(0, 0), self.at(0, 0), s, right)
            send(self.at(0, 1), self.at(0, 1), s + 1, left)
            send(self.at(0, 1), self.at(0, 1), s + 2, right)
            send(self.at(0, 0), self.at(0, 0), s + 3, left)

        def forward(self):
            s = self.slot
            arrive(self.at(3, 0), s)
            send(self.at(3, 0), self.at(3, 0), s + 4, ring_device(1))
            arrive(self.at(1, 1), s + 1)
            send(self.at(1, 1), self.at(1, 1), s + 5, ring_device(3))

        def near(self):
            arrive(self.at(3, 1), self.slot + 2)
            arrive(self.at(1, 0), self.slot + 3)

        def far(self):
            arrive(self.at(2, 0), self.slot + 4)
            arrive(self.at(2, 1), self.slot + 5)

    def swap(name, ref_at):
        extent, mine, at = axes[name]
        first = reserve(max(extent - 1, 0))
        for d in range(1, extent):
            send(ref_at(mine), ref_at(mine), first + d - 1, at(lax.rem(mine + d, extent)))

        def wait():
            for d in range(1, extent):
                arrive(ref_at(lax.rem(mine + extent - d, extent)), first + d - 1)

        return wait

    def columns(h):
        return slice(h * width, (h + 1) * width)

    def equal(a, b):
        return jnp.where(a == b, 1.0, 0.0).astype(BF16)

    def iota(shape, dim):
        return lax.broadcasted_iota(jnp.int32, shape, dim)

    def one_hots():
        size = (own, margin)
        identity = equal(iota((2 * margin,) * 2, 0), iota((2 * margin,) * 2, 1))
        for jj in range(RING):
            row = iota(size, 0) + jj * own
            pt_buf[jj, :, :margin] = equal(row_ref[0:1, :], row)
            pt_buf[jj, :, margin:] = equal(row_ref[1:2, :], row)
            p_buf[jj] = dot_nt(identity, pt_buf[jj]).astype(BF16)

    def order_weights():
        chunks, rows, lanes = weight_buf.shape
        select = equal(map_ref[...], iota((domains, domains), 0))
        ordered = dot(coarse_ref[...].reshape(rows * quarter, domains), select).astype(BF16)
        for chunk in range(chunks):
            owner = iota((domains, lanes), 1) // quarter + chunk * (lanes // quarter)
            wide = dot(ordered, equal(iota((domains, lanes), 0), owner))
            wide = wide.reshape(rows, quarter, lanes)
            size = (1, quarter, lanes)
            keep = iota(size, 1) == lax.rem(iota(size, 2), quarter)
            weight_buf[chunk] = jnp.sum(jnp.where(keep, wide, 0.0), axis=1).astype(BF16)

    def margin_columns():
        for source, target in ((k_buf, kp_buf), (a_buf, ap_buf)):
            total = dot(source[0], pt_buf[0])
            for jj in range(1, RING):
                total += dot(source[jj], pt_buf[jj])
            target[...] = total.astype(BF16)

    def own_basis():
        identity = equal(iota((own, own), 0), iota((own, own), 1))
        bt_buf[...] = dot_nt(identity, basis_ref[...]).astype(BF16)

    def basis_rows(jj):
        return basis_buf[jj, pl.ds(pl.multiple_of(j * quarter, quarter), quarter), :]

    def basis_terms():
        total = jnp.zeros((own, COARSE), F32)
        shared = jnp.zeros((2 * margin, COARSE), F32)
        rows = jnp.zeros((quarter, 2 * margin), F32)
        for jj in range(RING):
            total += dot_nt(k_buf[jj], basis_buf[jj])
            shared += dot_nt(p_buf[jj], basis_buf[jj])
            rows += dot(basis_rows(jj), pt_buf[jj])
        high = total.astype(BF16)
        kb_buf[0] = high
        kb_buf[1] = (total - high.astype(F32)).astype(BF16)
        pb_buf[...] = shared.astype(BF16)
        bp_buf[...] = rows.astype(BF16)

    def exchange_margins(step, h, values):
        margin_out[step, h, 0] = values[:margin].astype(BF16)
        margin_out[step, h, 1] = values[margin:].astype(BF16)
        first = reserve(2)
        send(margin_out.at[step, h, 1], margin_in.at[step, h, 0], first, domain_device(1))
        send(margin_out.at[step, h, 0], margin_in.at[step, h, 1], first + 1, domain_device(-1))

        def wait():
            arrive(margin_in.at[step, h, 0], first)
            arrive(margin_in.at[step, h, 1], first + 1)
            below, above = margin_in[step, h, 0], margin_in[step, h, 1]
            return masked(below, above)

        return wait

    def masked(below, above):
        zero = jnp.zeros_like(below)
        below = jnp.where(domain > 0, below, zero)
        above = jnp.where(domain < domains - 1, above, zero)
        return jnp.concatenate([below, above], axis=0)

    def process(h):
        cols = columns(h)
        gathered[0, h, j] = init_ref[:, cols].astype(BF16)
        gather = Gather(gathered.at[0, h], own)
        gather.start()
        sol_ref[:, cols] = init_ref[:, cols]
        yield "x0"

        def take_start(delta):
            defect[h] -= dot(k_buf[ring(delta)], gathered[0, h, ring(delta)])

        defect[h] = load_ref[:, cols] - dot(k_buf[j], gathered[0, h, j])
        gather.forward()
        yield "x1"
        gather.near()
        take_start(3)
        take_start(1)
        yield "x2"
        gather.far()
        take_start(2)

        for it in range(ITERS):
            level = 1 + 2 * it
            gathered[level, h, j] = defect[h].astype(BF16)
            gather = Gather(gathered.at[level, h], own)
            gather.start()
            yield "x3" if it == 0 else "u9"

            def take_defect(delta, first=False, level=level):
                jj = ring(delta)
                part = gathered[level, h, jj]
                terms = ((picked, dot(p_buf[jj], part)), (update, dot(a_buf[jj], part)))
                for target, term in terms:
                    if first:
                        target[h] = term
                    else:
                        target[h] += term

            take_defect(0, True)
            gather.forward()
            yield "e1"
            gather.near()
            take_defect(3)
            take_defect(1)
            yield "e2"
            gather.far()
            take_defect(2)
            margins = exchange_margins(2 * it, h, picked[h])
            yield "e3"
            result = dot(basis_rows(0), gathered[level, h, 0])
            for jj in range(1, RING):
                result += dot(basis_rows(jj), gathered[level, h, jj])
            shared = margins()
            result += dot(bp_buf[...], shared)
            coarse_all[it, h, z, y, c, x] = result.astype(BF16)
            wait = swap("z", lambda v: coarse_all.at[it, h, v, y, c, x])
            update[h] += dot(ap_buf[...], shared)
            level += 1
            gathered[level, h, j] = update[h].astype(BF16)
            gather = Gather(gathered.at[level, h], own)
            gather.start()
            yield "e4"

            def take_update(delta, first=False, level=level):
                jj = ring(delta)
                part = gathered[level, h, jj]
                term = dot(p_buf[jj], part)
                if first:
                    picked[h] = term
                else:
                    picked[h] += term
                defect[h] -= RELAX * dot(k_buf[jj], part)

            wait()
            wait = swap("y", lambda v: coarse_all.at[it, h, :, v, c, x])
            take_update(0, True)
            yield "u1"
            wait()
            wait = swap("x", lambda v: coarse_all.at[it, h, :, :, c, v])
            yield "u2"
            gather.forward()
            yield "u3"
            wait()
            wait = swap("c", lambda v: coarse_all.at[it, h, :, :, v])
            yield "u4"
            wait()
            everything = coarse_all[it, h].reshape(domains * quarter, width)
            chunks, _, lanes = weight_buf.shape
            partial = dot(weight_buf[0], everything[:lanes])
            for chunk in range(1, chunks):
                part = everything[chunk * lanes : (chunk + 1) * lanes]
                partial += dot(weight_buf[chunk], part)
            value_own[h] = partial
            value_out[it, h] = partial.astype(BF16)
            first = reserve(RING - 1)
            for d in (2, 1, 3):
                send(
                    value_out.at[it, h], value_in.at[it, h, d - 1], first + d - 1, ring_device(d)
                )
            yield "u5"
            gather.near()
            take_update(3)
            take_update(1)
            yield "u6"
            gather.far()
            take_update(2)
            yield "u7"
            total = value_own[h]
            for d in range(1, RING):
                arrive(value_in.at[it, h, d - 1], first + d - 1)
                total += value_in[it, h, d - 1].astype(F32)
            value = total.astype(BF16)
            margins = exchange_margins(2 * it + 1, h, picked[h] + dot(pb_buf[...], value))
            defect[h] -= RELAX * (dot(kb_buf[0], value) + dot(kb_buf[1], value))
            sol_ref[:, cols] += RELAX * (update[h] + dot(bt_buf[...], value))
            yield "u8"
            shared = margins()
            defect[h] -= RELAX * dot(kp_buf[...], shared)
            sol_ref[:, cols] += RELAX * dot(pt_buf[j], shared)

        mine = dot(p_buf[j], defect[h].astype(BF16))
        final_out[h, :, 0] = mine[:margin].reshape(RING, piece, width).astype(BF16)
        final_out[h, :, 1] = mine[margin:].reshape(RING, piece, width).astype(BF16)
        first = reserve(RING - 1)
        for d in (2, 1, 3):
            send(final_out.at[h, ring(d)], final_in.at[h, d - 1], first + d - 1, ring_device(d))
        yield "u9"
        total = final_out[h, j].astype(F32)
        for d in range(1, RING):
            arrive(final_in.at[h, d - 1], first + d - 1)
            total += final_in[h, d - 1].astype(F32)
        final_sum[h] = total.astype(BF16)
        first = reserve(2)
        send(final_sum.at[h, 1], final_all.at[h, j, 0], first, domain_device(1))
        send(final_sum.at[h, 0], final_all.at[h, j, 1], first + 1, domain_device(-1))
        yield "f1"
        arrive(final_all.at[h, j, 0], first)
        arrive(final_all.at[h, j, 1], first + 1)
        first = reserve(RING - 1)
        for d in (2, 1, 3):
            send(final_all.at[h, j], final_all.at[h, j], first + d - 1, ring_device(d))
        yield "f2"
        for d in range(1, RING):
            arrive(final_all.at[h, ring(RING - d)], first + d - 1)
        shared = masked(
            final_all[h, :, 0].reshape(margin, width), final_all[h, :, 1].reshape(margin, width)
        )
        res_ref[:, cols] = defect[h] + dot(pt_buf[j], shared)
        yield "f3"

    parts = {"A": process(0)}
    if PARTS > 1:
        parts["B"] = process(1)
    basis_gather = Gather(basis_buf, COARSE)

    def fetch_wait(first, last):
        for copy in copies[first:last]:
            copy.wait()

    def start_basis():
        basis_buf[j] = basis_ref[...]
        basis_gather.start()

    def end_basis():
        basis_gather.near()
        basis_gather.far()
        basis_terms()

    def matrices():
        fetch_wait(3, 3 + 2 * RING)
        margin_columns()
        own_basis()

    def weights():
        fetch_wait(3 + 2 * RING, 4 + 2 * RING)
        order_weights()

    extra = {
        "matrices": matrices,
        "start_basis": start_basis,
        "weights": weights,
        "forward_basis": basis_gather.forward,
        "end_basis": end_basis,
    }
    one_hots()
    fetch_wait(0, 3)
    pl.semaphore_wait(barrier, len(partners))
    for item in ORDER:
        if item in extra:
            extra[item]()
        elif item[0] in parts:
            if next(parts[item[0]]) != item[1:]:
                raise ValueError(item)
    for copy in started:
        copy.wait_send()


def on_device(
    stiffness, local_inverse, coarse_basis, coarse_inverse, loads, initial, margin_rows, coarse_map
):
    nz, ny, nc = SUB_EXTENTS
    nx = lax.axis_size("cr")
    own, block = stiffness.shape[1:]
    rhs = loads.shape[2]
    width = rhs // PARTS
    domains = coarse_map.shape[0]
    quarter = COARSE // RING
    margin = margin_rows.shape[2]
    piece = margin // RING
    lanes = min(256, domains * quarter)
    vmem = pl.BlockSpec(memory_space=pltpu.VMEM)
    hbm = pl.BlockSpec(memory_space=pl.ANY)
    slots = 256
    result = pl.pallas_call(
        functools.partial(kernel, (nz, ny, nc, nx)),
        out_shape=(
            jax.ShapeDtypeStruct((own, rhs), F32),
            jax.ShapeDtypeStruct((own, rhs), F32),
        ),
        in_specs=[hbm] * 6 + [vmem] * 2,
        out_specs=(vmem, vmem),
        scratch_shapes=[
            pltpu.VMEM((own, rhs), F32),
            pltpu.VMEM((own, rhs), F32),
            pltpu.VMEM((COARSE, own), BF16),
            pltpu.VMEM((COARSE, quarter, domains), BF16),
            pltpu.VMEM((domains * quarter // lanes, COARSE, lanes), BF16),
            pltpu.VMEM((RING, own, own), BF16),
            pltpu.VMEM((RING, own, own), BF16),
            pltpu.VMEM((RING, 2 * margin, own), BF16),
            pltpu.VMEM((RING, own, 2 * margin), BF16),
            pltpu.VMEM((own, 2 * margin), BF16),
            pltpu.VMEM((own, 2 * margin), BF16),
            pltpu.VMEM((quarter, 2 * margin), BF16),
            pltpu.VMEM((2 * margin, COARSE), BF16),
            pltpu.VMEM((2, own, COARSE), BF16),
            pltpu.VMEM((own, COARSE), BF16),
            pltpu.VMEM((RING, COARSE, own), BF16),
            pltpu.VMEM((1 + 2 * ITERS, PARTS, RING, own, width), BF16),
            pltpu.VMEM((PARTS, own, width), F32),
            pltpu.VMEM((PARTS, own, width), F32),
            pltpu.VMEM((PARTS, 2 * margin, width), F32),
            pltpu.VMEM((2 * ITERS, PARTS, 2, margin, width), BF16),
            pltpu.VMEM((2 * ITERS, PARTS, 2, margin, width), BF16),
            pltpu.VMEM((ITERS, PARTS, nz, ny, nc, nx, quarter, width), BF16),
            pltpu.VMEM((ITERS, PARTS, COARSE, width), BF16),
            pltpu.VMEM((PARTS, COARSE, width), F32),
            pltpu.VMEM((ITERS, PARTS, RING - 1, COARSE, width), BF16),
            pltpu.VMEM((PARTS, RING, 2, piece, width), BF16),
            pltpu.VMEM((PARTS, RING - 1, 2, piece, width), BF16),
            pltpu.VMEM((PARTS, 2, piece, width), BF16),
            pltpu.VMEM((PARTS, 2, piece, width), BF16),
            pltpu.VMEM((PARTS, RING, 2, piece, width), BF16),
            pltpu.SemaphoreType.DMA((4 + 2 * RING,)),
            pltpu.SemaphoreType.DMA((slots,)),
            pltpu.SemaphoreType.DMA((slots,)),
        ],
        compiler_params=pltpu.CompilerParams(
            collective_id=0, has_side_effects=True, vmem_limit_bytes=60 * 1024 * 1024
        ),
    )(
        stiffness[0],
        local_inverse[0],
        coarse_basis[0],
        coarse_inverse[0],
        loads[0],
        initial[0],
        margin_rows[0],
        coarse_map.reshape(1, domains),
    )
    return (result[0][None], result[1][None])


def solution(mesh):
    in_specs = (
        P(("sub", "cr"), "cc", None),
        P(("sub", "cr"), "cc", None),
        P(("sub", "cr"), None, "cc"),
        P(("sub", "cr"), None, "cc", None),
        P(("sub", "cr"), "cc", None),
        P(("sub", "cr"), "cc", None),
        P(("sub", "cr"), None, None),
        P(),
    )
    out_specs = (P(("sub", "cr"), "cc", None), P(("sub", "cr"), "cc", None))
    return jax.shard_map(
        on_device, mesh=mesh, in_specs=in_specs, out_specs=out_specs, check_vma=False
    )
```

```python
import functools

import jax
import jax.numpy as jnp
from jax import lax
from jax.experimental import pallas as pl
from jax.experimental.pallas import tpu as pltpu
from jax.sharding import PartitionSpec as P

COARSE = 64
ITERS = 2
RELAX = 0.5
PARTS = 2
SUB_EXTENTS = (4, 4, 2)
RING = 4
ORDER = (
    "Ax0", "matrices", "Ax1", "Bx0", "Ax2", "Bx1", "start_basis", "weights", "Ax3", "Ae1",
    "Bx2", "forward_basis", "Ae2", "Bx3", "Ae3", "end_basis", "Be1", "Ae4", "Au1", "Be2",
    "Be3", "Au2", "Au3", "Au4", "Au5", "Be4", "Bu1", "Au6", "Au7", "Bu2",
    "Au8", "Bu3", "Bu4", "Bu5", "Au9", "Bu6", "Bu7", "Bu8", "Ae1", "Bu9",
    "Ae2", "Ae3", "Be1", "Ae4", "Be2", "Au1", "Be3", "Au2", "Au3", "Be4",
    "Au4", "Bu1", "Au5", "Au6", "Bu2", "Bu3", "Au7", "Bu4", "Bu5", "Bu6",
    "Au8", "Bu7", "Bu8", "Au9", "Bu9", "Af1", "Bf1", "Af2", "Bf2", "Af3",
    "Bf3",
)
MESH = pl.DeviceIdType.MESH
BF16 = jnp.bfloat16
F32 = jnp.float32


def dot(a, b):
    return jnp.dot(a, b, preferred_element_type=F32)


def dot_nt(a, b):
    return lax.dot_general(a, b, (((1,), (1,)), ((), ())), preferred_element_type=F32)


def kernel(
    extents,
    stiff_hbm,
    inverse_hbm,
    basis_hbm,
    coarse_hbm,
    load_hbm,
    init_hbm,
    row_ref,
    map_ref,
    sol_ref,
    res_ref,
    load_ref,
    init_ref,
    basis_ref,
    coarse_ref,
    weight_buf,
    k_buf,
    a_buf,
    p_buf,
    pt_buf,
    ap_buf,
    kp_buf,
    bp_buf,
    pb_buf,
    kb_buf,
    bt_buf,
    basis_buf,
    gathered,
    defect,
    update,
    picked,
    margin_out,
    margin_in,
    coarse_all,
    value_out,
    value_own,
    value_in,
    final_out,
    final_in,
    final_sum,
    final_near,
    final_all,
    local_sem,
    send_sem,
    recv_sem,
):
    nz, ny, nc, nx = extents
    own, block = stiff_hbm.shape
    width = load_ref.shape[1] // PARTS
    margin = row_ref.shape[1]
    quarter = COARSE // RING
    piece = margin // RING
    sub = lax.axis_index("sub")
    x = lax.axis_index("cr")
    j = lax.axis_index("cc")
    z = sub // (ny * nc)
    y = lax.rem(sub // nc, ny)
    c = lax.rem(sub, nc)
    domain = sub * nx + x
    domains = nz * ny * nc * nx

    def device(zz, yy, cc, xx, jj):
        return ((zz * ny + yy) * nc + cc, xx, jj)

    def ring(delta):
        return lax.rem(j + delta, RING)

    def ring_device(delta):
        return device(z, y, c, x, ring(delta))

    def domain_device(delta):
        other = lax.rem(domain + delta + domains, domains)
        return (other // nx, lax.rem(other, nx), j)

    axes = {
        "z": (nz, z, lambda v: device(v, y, c, x, j)),
        "y": (ny, y, lambda v: device(z, v, c, x, j)),
        "x": (nx, x, lambda v: device(z, y, c, v, j)),
        "c": (nc, c, lambda v: device(z, y, v, x, j)),
    }

    partners = [ring_device(d) for d in range(1, RING)]
    partners += [domain_device(1), domain_device(-1)]
    for extent, mine, at in axes.values():
        partners += [at(lax.rem(mine + d, extent)) for d in range(1, extent)]

    copies = []

    def fetch(source, target):
        copy = pltpu.make_async_copy(source, target, local_sem.at[len(copies)])
        copy.start()
        copies.append(copy)

    barrier = pltpu.get_barrier_semaphore()
    for partner in partners:
        pl.semaphore_signal(barrier, inc=1, device_id=partner, device_id_type=MESH)
    fetch(init_hbm, init_ref)
    fetch(load_hbm, load_ref)
    fetch(basis_hbm, basis_ref)
    for source, target in ((stiff_hbm, k_buf), (inverse_hbm, a_buf)):
        for jj in range(RING):
            fetch(source.at[:, pl.ds(jj * own, own)], target.at[jj])
    fetch(coarse_hbm, coarse_ref)

    slots = [0]
    started = []

    def reserve(count):
        first = slots[0]
        slots[0] += count
        return first

    def remote(source, target, slot, to):
        return pltpu.make_async_remote_copy(
            src_ref=source,
            dst_ref=target,
            send_sem=send_sem.at[slot],
            recv_sem=recv_sem.at[slot],
            device_id=to,
            device_id_type=MESH,
        )

    def send(source, target, slot, to):
        copy = remote(source, target, slot, to)
        copy.start()
        started.append(copy)

    def arrive(landed, slot):
        remote(landed, landed, slot, ring_device(1)).wait_recv()

    class Gather:
        def __init__(self, ref, rows):
            self.ref, self.half, self.slot = ref, rows // 2, reserve(6)

        def at(self, delta, half):
            return self.ref.at[ring(delta), pl.ds(half * self.half, self.half)]

        def start(self):
            right, left, s = ring_device(1), ring_device(3), self.slot
            send(self.at(0, 0), self.at(0, 0), s, right)
            send(self.at(0, 1), self.at(0, 1), s + 1, left)
            send(self.at(0, 1), self.at(0, 1), s + 2, right)
            send(self.at(0, 0), self.at(0, 0), s + 3, left)

        def forward(self):
            s = self.slot
            arrive(self.at(3, 0), s)
            send(self.at(3, 0), self.at(3, 0), s + 4, ring_device(1))
            arrive(self.at(1, 1), s + 1)
            send(self.at(1, 1), self.at(1, 1), s + 5, ring_device(3))

        def near(self):
            arrive(self.at(3, 1), self.slot + 2)
            arrive(self.at(1, 0), self.slot + 3)

        def far(self):
            arrive(self.at(2, 0), self.slot + 4)
            arrive(self.at(2, 1), self.slot + 5)

    def swap(name, ref_at):
        extent, mine, at = axes[name]
        first = reserve(max(extent - 1, 0))
        for d in range(1, extent):
            send(ref_at(mine), ref_at(mine), first + d - 1, at(lax.rem(mine + d, extent)))

        def wait():
            for d in range(1, extent):
                arrive(ref_at(lax.rem(mine + extent - d, extent)), first + d - 1)

        return wait

    def columns(h):
        return slice(h * width, (h + 1) * width)

    def equal(a, b):
        return jnp.where(a == b, 1.0, 0.0).astype(BF16)

    def iota(shape, dim):
        return lax.broadcasted_iota(jnp.int32, shape, dim)

    def one_hots():
        size = (own, margin)
        identity = equal(iota((2 * margin,) * 2, 0), iota((2 * margin,) * 2, 1))
        for jj in range(RING):
            row = iota(size, 0) + jj * own
            pt_buf[jj, :, :margin] = equal(row_ref[0:1, :], row)
            pt_buf[jj, :, margin:] = equal(row_ref[1:2, :], row)
            p_buf[jj] = dot_nt(identity, pt_buf[jj]).astype(BF16)

    def order_weights():
        chunks, rows, lanes = weight_buf.shape
        select = equal(map_ref[...], iota((domains, domains), 0))
        ordered = dot(coarse_ref[...].reshape(rows * quarter, domains), select).astype(BF16)
        for chunk in range(chunks):
            owner = iota((domains, lanes), 1) // quarter + chunk * (lanes // quarter)
            wide = dot(ordered, equal(iota((domains, lanes), 0), owner))
            wide = wide.reshape(rows, quarter, lanes)
            size = (1, quarter, lanes)
            keep = iota(size, 1) == lax.rem(iota(size, 2), quarter)
            weight_buf[chunk] = jnp.sum(jnp.where(keep, wide, 0.0), axis=1).astype(BF16)

    def margin_columns():
        for source, target in ((k_buf, kp_buf), (a_buf, ap_buf)):
            total = dot(source[0], pt_buf[0])
            for jj in range(1, RING):
                total += dot(source[jj], pt_buf[jj])
            target[...] = total.astype(BF16)

    def own_basis():
        identity = equal(iota((own, own), 0), iota((own, own), 1))
        bt_buf[...] = dot_nt(identity, basis_ref[...]).astype(BF16)

    def basis_rows(jj):
        return basis_buf[jj, pl.ds(pl.multiple_of(j * quarter, quarter), quarter), :]

    def basis_terms():
        total = jnp.zeros((own, COARSE), F32)
        shared = jnp.zeros((2 * margin, COARSE), F32)
        rows = jnp.zeros((quarter, 2 * margin), F32)
        for jj in range(RING):
            total += dot_nt(k_buf[jj], basis_buf[jj])
            shared += dot_nt(p_buf[jj], basis_buf[jj])
            rows += dot(basis_rows(jj), pt_buf[jj])
        high = total.astype(BF16)
        kb_buf[0] = high
        kb_buf[1] = (total - high.astype(F32)).astype(BF16)
        pb_buf[...] = shared.astype(BF16)
        bp_buf[...] = rows.astype(BF16)

    def exchange_margins(step, h, values):
        margin_out[step, h, 0] = values[:margin].astype(BF16)
        margin_out[step, h, 1] = values[margin:].astype(BF16)
        first = reserve(2)
        send(margin_out.at[step, h, 1], margin_in.at[step, h, 0], first, domain_device(1))
        send(margin_out.at[step, h, 0], margin_in.at[step, h, 1], first + 1, domain_device(-1))

        def wait():
            arrive(margin_in.at[step, h, 0], first)
            arrive(margin_in.at[step, h, 1], first + 1)
            below, above = margin_in[step, h, 0], margin_in[step, h, 1]
            return masked(below, above)

        return wait

    def masked(below, above):
        zero = jnp.zeros_like(below)
        below = jnp.where(domain > 0, below, zero)
        above = jnp.where(domain < domains - 1, above, zero)
        return jnp.concatenate([below, above], axis=0)

    def process(h):
        cols = columns(h)
        gathered[0, h, j] = init_ref[:, cols].astype(BF16)
        gather = Gather(gathered.at[0, h], own)
        gather.start()
        sol_ref[:, cols] = init_ref[:, cols]
        yield "x0"

        def take_start(delta):
            defect[h] -= dot(k_buf[ring(delta)], gathered[0, h, ring(delta)])

        defect[h] = load_ref[:, cols] - dot(k_buf[j], gathered[0, h, j])
        gather.forward()
        yield "x1"
        gather.near()
        take_start(3)
        take_start(1)
        yield "x2"
        gather.far()
        take_start(2)

        for it in range(ITERS):
            level = 1 + 2 * it
            gathered[level, h, j] = defect[h].astype(BF16)
            gather = Gather(gathered.at[level, h], own)
            gather.start()
            yield "x3" if it == 0 else "u9"

            def take_defect(delta, first=False, level=level):
                jj = ring(delta)
                part = gathered[level, h, jj]
                terms = ((picked, dot(p_buf[jj], part)), (update, dot(a_buf[jj], part)))
                for target, term in terms:
                    if first:
                        target[h] = term
                    else:
                        target[h] += term

            take_defect(0, True)
            gather.forward()
            yield "e1"
            gather.near()
            take_defect(3)
            take_defect(1)
            yield "e2"
            gather.far()
            take_defect(2)
            margins = exchange_margins(2 * it, h, picked[h])
            yield "e3"
            result = dot(basis_rows(0), gathered[level, h, 0])
            for jj in range(1, RING):
                result += dot(basis_rows(jj), gathered[level, h, jj])
            shared = margins()
            result += dot(bp_buf[...], shared)
            coarse_all[it, h, z, y, c, x] = result.astype(BF16)
            wait = swap("z", lambda v: coarse_all.at[it, h, v, y, c, x])
            update[h] += dot(ap_buf[...], shared)
            level += 1
            gathered[level, h, j] = update[h].astype(BF16)
            gather = Gather(gathered.at[level, h], own)
            gather.start()
            yield "e4"

            def take_update(delta, first=False, level=level):
                jj = ring(delta)
                part = gathered[level, h, jj]
                term = dot(p_buf[jj], part)
                if first:
                    picked[h] = term
                else:
                    picked[h] += term
                defect[h] -= RELAX * dot(k_buf[jj], part)

            wait()
            low, high = pl.ds(0, nz // 2), pl.ds(nz // 2, nz - nz // 2)
            wait = swap("y", lambda v: coarse_all.at[it, h, low, v, c, x])
            other = swap("x", lambda v: coarse_all.at[it, h, high, y, c, v])
            take_update(0, True)
            yield "u1"
            wait()
            other()
            wait = swap("x", lambda v: coarse_all.at[it, h, low, :, c, v])
            other = swap("y", lambda v: coarse_all.at[it, h, high, v, c])
            yield "u2"
            gather.forward()
            yield "u3"
            wait()
            other()
            wait = swap("c", lambda v: coarse_all.at[it, h, :, :, v])
            yield "u4"
            wait()
            everything = coarse_all[it, h].reshape(domains * quarter, width)
            chunks, _, lanes = weight_buf.shape
            partial = dot(weight_buf[0], everything[:lanes])
            for chunk in range(1, chunks):
                part = everything[chunk * lanes : (chunk + 1) * lanes]
                partial += dot(weight_buf[chunk], part)
            value_own[h] = partial
            value_out[it, h] = partial.astype(BF16)
            first = reserve(RING - 1)
            for d in (2, 1, 3):
                send(
                    value_out.at[it, h], value_in.at[it, h, d - 1], first + d - 1, ring_device(d)
                )
            yield "u5"
            gather.near()
            take_update(3)
            take_update(1)
            yield "u6"
            gather.far()
            take_update(2)
            yield "u7"
            total = value_own[h]
            for d in range(1, RING):
                arrive(value_in.at[it, h, d - 1], first + d - 1)
                total += value_in[it, h, d - 1].astype(F32)
            value = total.astype(BF16)
            margins = exchange_margins(2 * it + 1, h, picked[h] + dot(pb_buf[...], value))
            defect[h] -= RELAX * (dot(kb_buf[0], value) + dot(kb_buf[1], value))
            sol_ref[:, cols] += RELAX * (update[h] + dot(bt_buf[...], value))
            yield "u8"
            shared = margins()
            defect[h] -= RELAX * dot(kp_buf[...], shared)
            sol_ref[:, cols] += RELAX * dot(pt_buf[j], shared)

        mine = dot(p_buf[j], defect[h].astype(BF16))
        final_out[h, :, 0] = mine[:margin].reshape(RING, piece, width).astype(BF16)
        final_out[h, :, 1] = mine[margin:].reshape(RING, piece, width).astype(BF16)
        first = reserve(RING - 1)
        for d in (2, 1, 3):
            send(final_out.at[h, ring(d)], final_in.at[h, d - 1], first + d - 1, ring_device(d))
        yield "u9"
        total = final_out[h, j].astype(F32)
        for d in range(1, RING):
            arrive(final_in.at[h, d - 1], first + d - 1)
            total += final_in[h, d - 1].astype(F32)
        final_sum[h] = total.astype(BF16)
        first = reserve(2)
        send(final_sum.at[h, 1], final_all.at[h, j, 0], first, domain_device(1))
        send(final_sum.at[h, 0], final_all.at[h, j, 1], first + 1, domain_device(-1))
        yield "f1"
        arrive(final_all.at[h, j, 0], first)
        arrive(final_all.at[h, j, 1], first + 1)
        first = reserve(RING - 1)
        for d in (2, 1, 3):
            send(final_all.at[h, j], final_all.at[h, j], first + d - 1, ring_device(d))
        yield "f2"
        for d in range(1, RING):
            arrive(final_all.at[h, ring(RING - d)], first + d - 1)
        shared = masked(
            final_all[h, :, 0].reshape(margin, width), final_all[h, :, 1].reshape(margin, width)
        )
        res_ref[:, cols] = defect[h] + dot(pt_buf[j], shared)
        yield "f3"

    parts = {"A": process(0)}
    if PARTS > 1:
        parts["B"] = process(1)
    basis_gather = Gather(basis_buf, COARSE)

    def fetch_wait(first, last):
        for copy in copies[first:last]:
            copy.wait()

    def start_basis():
        basis_buf[j] = basis_ref[...]
        basis_gather.start()

    def end_basis():
        basis_gather.near()
        basis_gather.far()
        basis_terms()

    def matrices():
        fetch_wait(3, 3 + 2 * RING)
        margin_columns()
        own_basis()

    def weights():
        fetch_wait(3 + 2 * RING, 4 + 2 * RING)
        order_weights()

    extra = {
        "matrices": matrices,
        "start_basis": start_basis,
        "weights": weights,
        "forward_basis": basis_gather.forward,
        "end_basis": end_basis,
    }
    one_hots()
    fetch_wait(0, 3)
    pl.semaphore_wait(barrier, len(partners))
    for item in ORDER:
        if item in extra:
            extra[item]()
        elif item[0] in parts:
            if next(parts[item[0]]) != item[1:]:
                raise ValueError(item)
    for copy in started:
        copy.wait_send()


def on_device(
    stiffness, local_inverse, coarse_basis, coarse_inverse, loads, initial, margin_rows, coarse_map
):
    nz, ny, nc = SUB_EXTENTS
    nx = lax.axis_size("cr")
    own, block = stiffness.shape[1:]
    rhs = loads.shape[2]
    width = rhs // PARTS
    domains = coarse_map.shape[0]
    quarter = COARSE // RING
    margin = margin_rows.shape[2]
    piece = margin // RING
    lanes = min(256, domains * quarter)
    vmem = pl.BlockSpec(memory_space=pltpu.VMEM)
    hbm = pl.BlockSpec(memory_space=pl.ANY)
    slots = 256
    result = pl.pallas_call(
        functools.partial(kernel, (nz, ny, nc, nx)),
        out_shape=(
            jax.ShapeDtypeStruct((own, rhs), F32),
            jax.ShapeDtypeStruct((own, rhs), F32),
        ),
        in_specs=[hbm] * 6 + [vmem] * 2,
        out_specs=(vmem, vmem),
        scratch_shapes=[
            pltpu.VMEM((own, rhs), F32),
            pltpu.VMEM((own, rhs), F32),
            pltpu.VMEM((COARSE, own), BF16),
            pltpu.VMEM((COARSE, quarter, domains), BF16),
            pltpu.VMEM((domains * quarter // lanes, COARSE, lanes), BF16),
            pltpu.VMEM((RING, own, own), BF16),
            pltpu.VMEM((RING, own, own), BF16),
            pltpu.VMEM((RING, 2 * margin, own), BF16),
            pltpu.VMEM((RING, own, 2 * margin), BF16),
            pltpu.VMEM((own, 2 * margin), BF16),
            pltpu.VMEM((own, 2 * margin), BF16),
            pltpu.VMEM((quarter, 2 * margin), BF16),
            pltpu.VMEM((2 * margin, COARSE), BF16),
            pltpu.VMEM((2, own, COARSE), BF16),
            pltpu.VMEM((own, COARSE), BF16),
            pltpu.VMEM((RING, COARSE, own), BF16),
            pltpu.VMEM((1 + 2 * ITERS, PARTS, RING, own, width), BF16),
            pltpu.VMEM((PARTS, own, width), F32),
            pltpu.VMEM((PARTS, own, width), F32),
            pltpu.VMEM((PARTS, 2 * margin, width), F32),
            pltpu.VMEM((2 * ITERS, PARTS, 2, margin, width), BF16),
            pltpu.VMEM((2 * ITERS, PARTS, 2, margin, width), BF16),
            pltpu.VMEM((ITERS, PARTS, nz, ny, nc, nx, quarter, width), BF16),
            pltpu.VMEM((ITERS, PARTS, COARSE, width), BF16),
            pltpu.VMEM((PARTS, COARSE, width), F32),
            pltpu.VMEM((ITERS, PARTS, RING - 1, COARSE, width), BF16),
            pltpu.VMEM((PARTS, RING, 2, piece, width), BF16),
            pltpu.VMEM((PARTS, RING - 1, 2, piece, width), BF16),
            pltpu.VMEM((PARTS, 2, piece, width), BF16),
            pltpu.VMEM((PARTS, 2, piece, width), BF16),
            pltpu.VMEM((PARTS, RING, 2, piece, width), BF16),
            pltpu.SemaphoreType.DMA((4 + 2 * RING,)),
            pltpu.SemaphoreType.DMA((slots,)),
            pltpu.SemaphoreType.DMA((slots,)),
        ],
        compiler_params=pltpu.CompilerParams(
            collective_id=0, has_side_effects=True, vmem_limit_bytes=60 * 1024 * 1024
        ),
    )(
        stiffness[0],
        local_inverse[0],
        coarse_basis[0],
        coarse_inverse[0],
        loads[0],
        initial[0],
        margin_rows[0],
        coarse_map.reshape(1, domains),
    )
    return (result[0][None], result[1][None])


def solution(mesh):
    in_specs = (
        P(("sub", "cr"), "cc", None),
        P(("sub", "cr"), "cc", None),
        P(("sub", "cr"), None, "cc"),
        P(("sub", "cr"), None, "cc", None),
        P(("sub", "cr"), "cc", None),
        P(("sub", "cr"), "cc", None),
        P(("sub", "cr"), None, None),
        P(),
    )
    out_specs = (P(("sub", "cr"), "cc", None), P(("sub", "cr"), "cc", None))
    return jax.shard_map(
        on_device, mesh=mesh, in_specs=in_specs, out_specs=out_specs, check_vma=False
    )
```
